32 devices in a mesh: groups: 2 (over x), row: 16 (over z, y, core).
Axes of the slice: x: 2, y: 2, z: 4, core: 2. Of those that a mesh axis runs over, the one named last changes fastest.
Arguments:
- a_blocks: float32 [192, 12, 128, 128], P(('groups', 'row')), parts along dimension 0, may hold values from -0.15625 to 0.15625
- b_blocks: float32 [192, 12, 128, 128], P(('groups', 'row')), parts along dimension 0, may hold values from -6 to 6
- a_columns: int32 [192, 12], P(('groups', 'row')), parts along dimension 0, may hold values from 0 to 95, as said below
- b_columns: int32 [192, 12], P(('groups', 'row')), parts along dimension 0, may hold values from 0 to 95, as said below
- c_columns: int32 [192, 12], P(('groups', 'row')), parts along dimension 0, may hold values from 0 to 95, as said below
Outputs:
- c_blocks: float32 [192, 12, 128, 128], P(('groups', 'row')), parts along dimension 0
The draws below stay inside these ranges and needn't reach their ends.
There are 2 independent parts, one for each index of `groups`. The reference program is written for one: setup_inputs(seed, part) draws one part's arguments, and reference() takes and returns one part's arrays. A program takes and returns all parts, laid end to end along the dimension named above; each array names one. Nothing has to cross between parts.
Inputs may be any that keep to these rules, and one draw needn't show every extreme that they name: `a_columns`: block columns of one block row are distinct, include the row's own index, and lie within 12 of the row's index around the periodic cycle of 96 block indices. `b_columns`: block columns of one block row are distinct, include the row's own index, and lie within 12 of the row's index around the periodic cycle of 96 block indices. `c_columns`: block columns of one block row are distinct, include the row's own index, and lie within 12 of the row's index around the periodic cycle of 96 block indices.
All inputs are finite; a program needn't handle non-finite values.
Results may differ from the reference program's by a relative error of at most 0.0003.
Values sent between devices are 32-bit elements; how exact they have to be, the bound alone decides.
No kernel may reach another device: no remote copies, remote signals or barrier semaphores. Data moves between devices by JAX's collectives and lax.ppermute only.
A program may use at most 128 MiB of HBM per device.

```python
import jax
import jax.numpy as jnp
from jax import lax

BS = 128
RD = 6
KA = 12
KB = 12
KC = 12
NB = 96


def band_columns(key, count):
    reach = 2 * RD
    spread = 2 * reach
    scores = jax.random.randint(key, (NB, spread), 0, 1 << 20) * spread + jnp.arange(spread, dtype=jnp.int32)[None, :]
    order = jnp.argsort(scores, axis=1)[:, :count - 1].astype(jnp.int32)
    offsets = jnp.where(order < reach, order - reach, order - reach + 1)
    offsets = jnp.concatenate([jnp.zeros((NB, 1), jnp.int32), offsets], axis=1)
    return ((jnp.arange(NB, dtype=jnp.int32)[:, None] + offsets) % NB).astype(jnp.int32)


def draw_a_columns(key, part):
    key = jax.random.fold_in(key, 11)
    return band_columns(key, KA)


def draw_b_columns(key, part):
    key = jax.random.fold_in(key, 23)
    return band_columns(key, KB)


def draw_c_columns(key, part):
    key = jax.random.fold_in(key, 37)
    return band_columns(key, KC)


def levels(rng, shape, split, low, largest):
    loudness, own = 1.0, jax.random.fold_in(rng, 6)
    for dim, shards_of in split:
        heights = jnp.exp(jax.random.uniform(jax.random.fold_in(own, dim), (shards_of,), jnp.float32, low / len(split), largest / len(split)))
        loudness = loudness * jnp.repeat(heights, shape[dim] // shards_of).reshape([-1 if axis == dim else 1 for axis in range(len(shape))])
    return loudness


def noise(key, dims, scale, limit, pieces=(), held_as=jnp.bfloat16):
    values = scale * jax.random.normal(key, dims, jnp.float32)
    if pieces:
        values = values * levels(key, dims, pieces, -0.22, 0.18)
    return jnp.clip(values, -limit, limit).astype(held_as)


def setup_inputs(seed: int = 0, part: int = 0) -> dict:
    key_list = jax.random.split(jax.random.key(seed), 6)
    part_splits = jax.random.split(jax.random.fold_in(key_list[5], part), 6)
    a_blocks = noise(part_splits[0], (NB, KA, BS, BS), (BS * KA) ** -0.5, 0.15625, ((0, 16),), jnp.float32)
    b_blocks = noise(part_splits[1], (NB, KB, BS, BS), 1.0, 6.0, ((0, 16),), jnp.float32)
    a_columns = draw_a_columns(jax.random.fold_in(jax.random.fold_in(key_list[5], part), 71), part)
    b_columns = draw_b_columns(jax.random.fold_in(jax.random.fold_in(key_list[5], part), 71), part)
    c_columns = draw_c_columns(jax.random.fold_in(jax.random.fold_in(key_list[5], part), 71), part)
    return {"a_blocks": a_blocks, "b_blocks": b_blocks, "a_columns": a_columns, "b_columns": b_columns, "c_columns": c_columns}


def reference(a_blocks, b_blocks, a_columns, b_columns, c_columns):
    def row_product(inputs):
        left_row, column_row, target_row = inputs
        picked = jnp.take(b_blocks, column_row, axis=0)
        picked_columns = jnp.take(b_columns, column_row, axis=0)
        matches = (picked_columns[:, :, None] == target_row[None, None, :]).astype(jnp.float32)
        selected = jnp.einsum("abs,abxy->asxy", matches, picked, precision=lax.Precision.HIGHEST)
        return jnp.einsum("axy,asyz->sxz", left_row, selected, precision=lax.Precision.HIGHEST)

    return lax.map(row_product, (a_blocks, a_columns, c_columns))
```

```python
import functools

import jax
import jax.numpy as jnp
from jax import lax
from jax.experimental import pallas as pl
from jax.experimental.pallas import tpu as pltpu
from jax.sharding import PartitionSpec as P

UNROLL = 4
VMEM_BYTES = 48 * 1024 * 1024
OWN, MATE, CROSS, PAIR, FAR = range(5)
SLICES = (6, 12, 12, 12, 12, 12, 6)


def stage_plan(blocks):
    unit = sum(SLICES)
    cuts = [0]
    for size in SLICES:
        cuts.append(cuts[-1] + blocks * size // unit)
    pieces = list(zip(cuts[:-1], [b - a for a, b in zip(cuts[:-1], cuts[1:])]))

    def piece(region, n):
        return (region,) + pieces[n]

    stages = [
        [(OWN, 0, blocks)],
        [(MATE, 0, blocks)],
        [piece(PAIR, 0), piece(PAIR, 1), piece(FAR, 0), piece(CROSS, 0)],
        [piece(PAIR, 2), piece(PAIR, 3), piece(FAR, 1), piece(FAR, 2), piece(CROSS, 1), piece(CROSS, 2)],
        [piece(PAIR, 4), piece(PAIR, 5), piece(FAR, 3), piece(FAR, 4), piece(CROSS, 3), piece(CROSS, 4)],
        [piece(PAIR, 6), piece(FAR, 5), piece(CROSS, 5)],
        [piece(FAR, 6), piece(CROSS, 6)],
    ]
    return pieces, stages


def list_layout(stages, rows):
    starts, at = [], 0
    for stage in stages:
        starts.append(at)
        at += sum(size for _, _, size in stage) * rows + UNROLL
    return starts, at


def list_kernel(stages, starts, rows, ka, kb, kc, info, a_cols, c_cols, b_cols, work, counts, where_a, where_c):
    first, total = info[0], info[1]
    pool = 5 * rows
    reach = 2 * rows
    span = pool + 2 * reach

    def wrapped(value):
        value = jnp.where(value < 0, value + total, value)
        return jnp.where(value >= total, value - total, value)

    def clear_a(n, _):
        where_a[n] = -1
        return 0

    def clear_c(n, _):
        where_c[n] = -1
        return 0

    lax.fori_loop(0, rows * pool, clear_a, 0)
    lax.fori_loop(0, rows * span, clear_c, 0)

    def note(i, _):
        for slot in range(ka):
            where_a[i * pool + wrapped(a_cols[i, slot] - first + reach)] = slot
        for slot in range(kc):
            where_c[i * span + wrapped(c_cols[i, slot] - first + 2 * reach)] = slot
        return 0

    lax.fori_loop(0, rows, note, 0)

    place = {}
    for number, stage in enumerate(stages):
        counts[number] = 0
        at = 0
        for region, begin, size in stage:
            for n in range(begin, begin + size):
                place[region, n] = (number, at + n - begin)
            at += size

    for region in range(5):
        group = info[2 + region]
        for row in range(rows):
            q = group * rows + row

            def each(i, _, region=region, group=group, row=row, q=q):
                slot = where_a[i * pool + q]

                @pl.when(slot >= 0)
                def _():
                    for b in range(kb):
                        number, index = place[region, row * kb + b]
                        column = wrapped(b_cols[q * kb + b] - first + 2 * reach)
                        target = where_c[i * span + column]
                        count = counts[number]
                        work[starts[number] + count] = (
                            (i * ka + slot) + (i * kc + target) * 256 + index * 65536
                        )
                        counts[number] = count + jnp.where(target >= 0, 1, 0)

                return 0

            lax.fori_loop(0, rows, each, 0)
    for number in range(len(stages)):
        for n in range(UNROLL):
            work[starts[number] + counts[number] + n] = rows * kc * 256


def make_lists(stages, rows, ka, kb, kc, info, a_cols, c_cols, b_cols):
    starts, size = list_layout(stages, rows)
    smem = pl.BlockSpec(memory_space=pltpu.SMEM)
    return pl.pallas_call(
        functools.partial(list_kernel, stages, starts, rows, ka, kb, kc),
        out_shape=(
            jax.ShapeDtypeStruct((size,), jnp.int32),
            jax.ShapeDtypeStruct((len(stages),), jnp.int32),
        ),
        in_specs=[smem] * 4,
        out_specs=(smem, smem),
        scratch_shapes=[
            pltpu.SMEM((rows * 5 * rows,), jnp.int32),
            pltpu.SMEM((rows * 9 * rows,), jnp.int32),
        ],
        name="work_lists",
    )(info, a_cols, c_cols, b_cols)


def product(a, b):
    a_high = a.astype(jnp.bfloat16)
    a_low = (a - a_high.astype(jnp.float32)).astype(jnp.bfloat16)
    b_high = b.astype(jnp.bfloat16)
    b_low = (b - b_high.astype(jnp.float32)).astype(jnp.bfloat16)
    dot = functools.partial(jnp.dot, preferred_element_type=jnp.float32)
    return dot(a_high, b_high) + (dot(a_low, b_high) + dot(a_high, b_low))


def stage_kernel(number, start, sizes, fresh, work, counts, a_hbm, *refs):
    b_hbms, refs = refs[: len(sizes)], refs[len(sizes) :]
    if not fresh:
        c_in, refs = refs[0], refs[1:]
    c_out, a_v, b_v, c_v, sems = refs
    blocks = c_out.shape[0]
    copies = [pltpu.make_async_copy(a_hbm, a_v, sems.at[0])]
    at = 0
    for n, size in enumerate(sizes):
        copies.append(pltpu.make_async_copy(b_hbms[n], b_v.at[pl.ds(at, size)], sems.at[2 + n]))
        at += size
    if not fresh:
        copies.append(pltpu.make_async_copy(c_in, c_v.at[pl.ds(0, blocks)], sems.at[1]))
    for copy in copies:
        copy.start()
    if fresh:
        def zero(n, _):
            c_v[n] = jnp.zeros(c_v.shape[1:], jnp.float32)
            return 0

        lax.fori_loop(0, blocks, zero, 0)
    for copy in copies:
        copy.wait()

    def step(n, _):
        results = []
        for u in range(UNROLL):
            code = work[start + n * UNROLL + u]
            a = a_v[code & 255]
            b = b_v[code >> 16]
            results.append(((code >> 8) & 255, product(a, b)))
        for target, value in results:
            c_v[target] += value
        return 0

    lax.fori_loop(0, (counts[number] + UNROLL - 1) // UNROLL, step, 0)
    out = pltpu.make_async_copy(c_v.at[pl.ds(0, blocks)], c_out, sems.at[1])
    out.start()
    out.wait()


def run_stage(number, start, work, counts, a, pieces, c):
    sizes = [p.shape[0] for p in pieces]
    smem = pl.BlockSpec(memory_space=pltpu.SMEM)
    hbm = pl.BlockSpec(memory_space=pl.ANY)
    fresh = c is None
    shape = a.shape
    operands = [work, counts, a, *pieces] + ([] if fresh else [c])
    return pl.pallas_call(
        functools.partial(stage_kernel, number, start, sizes, fresh),
        out_shape=jax.ShapeDtypeStruct(shape, jnp.float32),
        in_specs=[smem, smem] + [hbm] * (len(operands) - 2),
        out_specs=hbm,
        scratch_shapes=[
            pltpu.VMEM(shape, jnp.float32),
            pltpu.VMEM((sum(sizes),) + shape[1:], jnp.float32),
            pltpu.VMEM((shape[0] + 1,) + shape[1:], jnp.float32),
            pltpu.SemaphoreType.DMA((2 + len(sizes),)),
        ],
        input_output_aliases={} if fresh else {len(operands) - 1: 0},
        compiler_params=pltpu.CompilerParams(vmem_limit_bytes=VMEM_BYTES),
        cost_estimate=pl.CostEstimate(
            flops=4_000_000_000, bytes_accessed=20_000_000, transcendentals=0
        ),
        name=f"products_{number}",
    )(*operands)


def passed_along(block, axis, distance):
    devices = range(lax.axis_size(axis))
    route = [((i - distance) % len(devices), i) for i in devices]
    return lax.ppermute(block, axis, route)


def local(a_blocks, b_blocks, a_columns, b_columns, c_columns):
    rows, ka = a_columns.shape
    kb, kc = b_columns.shape[1], c_columns.shape[1]
    devices = lax.axis_size("row")
    block = a_blocks.shape[2:]
    me = lax.axis_index("row")
    even_chip, core = (me // 2) % 2 == 0, me % 2

    pair_route = [(i, i ^ 2) for i in range(devices)]
    mate_route = [(i, i ^ 1) for i in range(devices)]
    far_route = [(i, (i + 4 if (i // 2) % 2 == 0 else i - 4) % devices) for i in range(devices)]

    a = a_blocks.reshape((rows * ka,) + block)
    own = b_blocks.reshape((rows * kb,) + block)
    pieces, stages = stage_plan(rows * kb)
    starts, _ = list_layout(stages, rows)

    def cut(array, n):
        return lax.slice_in_dim(array, pieces[n][0], sum(pieces[n]), axis=0)

    first = cut(own, 0)
    first, rest = lax.optimization_barrier((first, own))
    pair = [lax.ppermute(first, "row", pair_route)]
    pair += [lax.ppermute(cut(rest, n), "row", pair_route) for n in range(1, len(pieces))]
    mate = lax.ppermute(own, "row", mate_route)
    columns = [passed_along(b_columns, "row", step) for step in (2, 1, -1, -2)]
    columns = jnp.concatenate(columns[:2] + [b_columns] + columns[2:], axis=0).reshape(-1)

    pair_group = jnp.where(even_chip, 4, 0)
    far_group = 4 - pair_group
    mate_group = jnp.where(core == 0, 3, 1)
    cross_group = 4 - mate_group
    info = jnp.stack(
        [me * rows, jnp.int32(rows * devices), jnp.int32(2), mate_group, cross_group, pair_group, far_group]
    ).astype(jnp.int32)
    work, counts = make_lists(stages, rows, ka, kb, kc, info, a_columns, c_columns, columns)

    far = [lax.ppermute(p, "row", far_route) for p in pair]
    send_pair = even_chip == (core == 0)
    cross = [
        lax.ppermute(jnp.where(send_pair, p, f), "row", mate_route) for p, f in zip(pair, far)
    ]
    arrived = {(OWN, 0): own, (MATE, 0): mate}
    for n, (begin, _) in enumerate(pieces):
        arrived[PAIR, begin], arrived[FAR, begin], arrived[CROSS, begin] = pair[n], far[n], cross[n]

    c = None
    for number, stage in enumerate(stages):
        c = run_stage(
            number, starts[number], work, counts, a, [arrived[r, begin] for r, begin, _ in stage], c
        )
    return c.reshape((rows, kc) + block)


def solution(mesh):
    return jax.shard_map(
        local,
        mesh=mesh,
        in_specs=(
            P(("groups", "row"), None, None, None),
            P(("groups", "row"), None, None, None),
            P(("groups", "row"), None),
            P(("groups", "row"), None),
            P(("groups", "row"), None),
        ),
        out_specs=P(("groups", "row"), None, None, None),
        check_vma=False,
    )
```

```python
import functools

import jax
import jax.numpy as jnp
from jax import lax
from jax.experimental import pallas as pl
from jax.experimental.pallas import tpu as pltpu
from jax.sharding import PartitionSpec as P

UNROLL = 8
VMEM_BYTES = 62 * 1024 * 1024
OWN, MATE, CROSS, PAIR, FAR = range(5)
SIZES = (8,) * 9
RAW = 2
NOTE = 8
KERNEL_BYTES = 9_000_000_000
BEAT7 = 0.05
CROSSES = (0, 3, 5, 7, 9)


def cut_up(blocks):
    unit = sum(SIZES)
    cuts = [0]
    for size in SIZES:
        cuts.append(cuts[-1] + blocks * size // unit)
    return [(a, b - a) for a, b in zip(cuts[:-1], cuts[1:])]


def fill(ref, begin, size, value):
    for n in range(begin, begin + size):
        ref[n] = value


def note_columns(rows, ka, kc, ac, where):
    span = 5 * rows
    reach = 2 * rows
    starts = (0, span * rows, 2 * span * rows, 2 * span * rows + span)
    fill(where, 0, 2 * span * rows, -65536 * 16384)
    fill(where, starts[2], 2 * span + 2 * reach, 0)

    def note(i, _):
        bit = 1 << i
        for slot in range(ka):
            q = ac[i * ka + slot]
            where[q * rows + i] = i * ka + slot
            where[starts[2] + q] = where[starts[2] + q] | bit
        for slot in range(kc):
            q = ac[rows * ka + i * kc + slot]
            where[starts[1] + q * rows + i] = (i * kc + slot) * 256
            where[starts[3] + reach + q] = where[starts[3] + reach + q] | bit
        return 0

    lax.fori_loop(0, rows, note, 0)


def pack_kernel(rows, ka, kb, kc, pieces, info, ac, mine, far_ac, near_ac, own, *refs):
    outs, (over, where, held, note_v, lefts, wanted, need, order, sems) = refs[:-9], refs[-9:]
    height = own.shape[1]
    load = pltpu.make_async_copy(own, held, sems.at[1])
    load.start()
    even, near = info[0], info[1]
    reach = 2 * rows
    span = 5 * rows
    total = rows * kb
    raw = pieces[RAW][0]
    kept = pieces[-1][0]
    side = 1 - 2 * even

    for hop, (other, used) in enumerate(((far_ac, 1), (near_ac, near))):
        offset = (2 - hop) * side * rows
        fill(lefts, 0, span, 0)
        fill(wanted, 0, span + 2 * reach, 0)

        def note(i, _, other=other):
            bit = 1 << i
            for slot in range(ka):
                at = other[i * ka + slot]
                lefts[at] = lefts[at] | bit
            for slot in range(kc):
                at = other[rows * ka + i * kc + slot] + reach
                wanted[at] = wanted[at] | bit
            return 0

        lax.fori_loop(0, rows, note, 0)

        def look(k, _, hop=hop, offset=offset, used=used):
            left = lefts[k + reach - offset] * used
            for b in range(kb):
                hit = left & wanted[reach + mine[k * kb + b] - offset]
                need[k * kb + b] = hit if hop == 0 else need[k * kb + b] | hit
            return 0

        lax.fori_loop(0, rows, look, 0)

    raw_base = (1 - even) * (total - raw)
    base = even * raw

    def keep(n, _):
        order[n] = raw_base + n
        return 0

    lax.fori_loop(0, raw, keep, 0)

    def sort(n, count):
        found = need[base + n] != 0
        place = jnp.where(found, raw + count, total - 1 - (n - count))
        order[place] = base + n
        return count + jnp.where(found, 1, 0)

    count = lax.fori_loop(0, total - raw, sort, 0)
    over[0] = jnp.where(count > kept - raw, 1, 0)

    load.wait()
    for out, (begin, size) in zip(outs, pieces[RAW:]):
        def start(n, _, out=out, begin=begin):
            pltpu.make_async_copy(
                held.at[order[begin + n]], out.at[pl.ds(n * height, height)], sems.at[0]
            ).start()
            return 0

        lax.fori_loop(0, size, start, 0)

    lane = lax.broadcasted_iota(jnp.int32, note_v.shape, 1)

    def write(n, values):
        block = order[n]
        entry = (block // kb) * 64 + mine[block]
        return jnp.where(lane == n, entry.astype(jnp.float32), values)

    note_v[...] = lax.fori_loop(0, total, write, jnp.zeros(note_v.shape, jnp.float32))
    tail = outs[0].at[pl.ds(pieces[RAW][1] * height, NOTE)]
    note_copy = pltpu.make_async_copy(note_v, tail, sems.at[2])
    note_copy.start()
    note_columns(rows, ka, kc, ac, where)
    for out, (begin, size) in zip(outs, pieces[RAW:]):
        def wait(n, _, out=out):
            pltpu.make_async_copy(held.at[0], out.at[pl.ds(0, height)], sems.at[0]).wait()
            return 0

        lax.fori_loop(0, size, wait, 0)
    note_copy.wait()


def pack(rows, ka, kb, kc, pieces, info, ac, mine, far_ac, near_ac, own):
    smem = pl.BlockSpec(memory_space=pltpu.SMEM)
    hbm = pl.BlockSpec(memory_space=pl.ANY)
    block = own.shape[1:]
    outs = pl.pallas_call(
        functools.partial(pack_kernel, rows, ka, kb, kc, pieces),
        out_shape=[
            jax.ShapeDtypeStruct((size * block[0] + (NOTE if n == 0 else 0), block[1]), own.dtype)
            for n, (_, size) in enumerate(pieces[RAW:])
        ]
        + [
            jax.ShapeDtypeStruct((1,), jnp.int32),
            jax.ShapeDtypeStruct((10 * rows * rows + 14 * rows,), jnp.int32),
        ],
        in_specs=[smem] * 5 + [hbm],
        out_specs=[hbm] * len(pieces[RAW:]) + [smem] * 2,
        scratch_shapes=[
            pltpu.VMEM(own.shape, own.dtype),
            pltpu.VMEM((NOTE, block[1]), jnp.float32),
            pltpu.SMEM((5 * rows,), jnp.int32),
            pltpu.SMEM((9 * rows,), jnp.int32),
            pltpu.SMEM((rows * kb,), jnp.int32),
            pltpu.SMEM((rows * kb,), jnp.int32),
            pltpu.SemaphoreType.DMA((3,)),
        ],
        compiler_params=pltpu.CompilerParams(vmem_limit_bytes=VMEM_BYTES),
        cost_estimate=pl.CostEstimate(
            flops=KERNEL_BYTES, bytes_accessed=1000, transcendentals=0
        ),
        name="order_blocks",
    )(info, ac, mine, far_ac, near_ac, own)
    return outs[:-2], outs[-2], outs[-1]


def split(x):
    high = x.astype(jnp.bfloat16)
    return high, (x - high.astype(jnp.float32)).astype(jnp.bfloat16)


def product(a, b):
    a_high, a_low = split(a)
    b_high, b_low = split(b)
    left = jnp.concatenate([a_high, a_low], axis=1)
    right = jnp.concatenate(
        [
            jnp.concatenate([b_high, b_low], axis=1),
            jnp.concatenate([b_high, jnp.zeros_like(b_low)], axis=1),
        ],
        axis=0,
    )
    both = jnp.dot(left, right, preferred_element_type=jnp.float32)
    return both[:, : b.shape[1]] + both[:, b.shape[1] :]


def stage_kernel(rows, ka, kb, kc, stage, fresh, part, clock, info, where, *refs):
    regions = sorted({region for region, _, _ in stage})
    tables = dict(zip(regions, refs[: len(regions)]))
    refs = refs[len(regions) :]
    a_hbm, b_hbms = refs[0], refs[1 : 1 + len(stage)]
    refs = refs[1 + len(stage) :]
    if not fresh:
        c_in, refs = refs[0], refs[1:]
    c_out, a_v, b_v, c_v, work, marks, sems = refs
    reach = 2 * rows
    span = 5 * rows
    a_blocks, c_blocks = rows * ka, rows * kc
    height = a_v.shape[1]
    pair_side = (2 * info[0] - 1) * 2
    mate_side = 1 - 2 * info[2]
    offsets = {OWN: 0, MATE: mate_side, CROSS: -mate_side, PAIR: pair_side, FAR: -pair_side}

    copies = []
    if not part:
        copies.append(pltpu.make_async_copy(a_hbm, a_v, sems.at[0]))
        if not fresh:
            copies.append(pltpu.make_async_copy(c_in, c_v.at[pl.ds(0, c_blocks)], sems.at[1]))
    at = 0
    for n, (_, _, size) in enumerate(stage):
        copies.append(
            pltpu.make_async_copy(
                b_hbms[n].at[pl.ds(0, size * height)],
                b_v.at[pl.ds(at * height, size * height)],
                sems.at[2 + n],
            )
        )
        at += size
    for copy in copies:
        copy.start()

    if part:
        fill(marks, 0, a_blocks + c_blocks + 2, 0)

    lefts, wanted = 2 * span * rows, 2 * span * rows + span
    count = 0
    at = 0
    for region, begin, size in stage:
        table, shift = tables[region], offsets[region] * rows + reach

        def look(n, count, table=table, shift=shift, begin=begin, at=at):
            entry = table[begin + n]
            q = (entry >> 6) + shift
            j = (entry & 63) + shift
            if fresh:
                c_v[at + n] = jnp.zeros(c_v.shape[1:], jnp.float32)

            def append(count):
                row, column = q * rows, span * rows + (j - reach) * rows
                place = (at + n) * 65536
                for i in range(rows):
                    left, target = where[row + i], where[column + i]
                    code = left + target + place
                    found = jnp.where((left | target) >= 0, 1, 0)
                    work[count] = code
                    count = count + found
                    if part:
                        marks[jnp.where(found != 0, left, a_blocks)] = 1
                        marks[jnp.where(found != 0, target >> 8, c_blocks) + a_blocks + 1] = 1
                return count

            hits = where[lefts + q] & where[wanted + j]
            return lax.cond(hits != 0, append, lambda count: count, count)

        count = lax.fori_loop(0, size, look, count)
        at += size
    for n in range(UNROLL):
        work[count + n] = c_blocks * 256

    def marked(begin, size, action):
        def one(n, _):
            @pl.when(marks[begin + n] != 0)
            def _():
                action(n)

            return 0

        lax.fori_loop(0, size, one, 0)

    def a_copy(n):
        return pltpu.make_async_copy(a_hbm.at[n], a_v.at[n], sems.at[0])

    def c_copy(n):
        return pltpu.make_async_copy(c_in.at[n], c_v.at[n], sems.at[1])

    def back_copy(n):
        return pltpu.make_async_copy(c_v.at[n], c_out.at[n], sems.at[1])

    if part:
        marked(0, a_blocks, lambda n: a_copy(n).start())
        marked(a_blocks + 1, c_blocks, lambda n: c_copy(n).start())
    for copy in copies:
        copy.wait()
    if part:
        marked(0, a_blocks, lambda n: a_copy(n).wait())
        marked(a_blocks + 1, c_blocks, lambda n: c_copy(n).wait())

    def step(n, _):
        results = []
        for u in range(UNROLL):
            code = work[n * UNROLL + u]
            b = b_v[pl.ds(pl.multiple_of((code >> 16) * height, height), height)]
            results.append(((code >> 8) & 255, product(a_v[code & 255], b)))
        for target, value in results:
            c_v[target] += value
        return 0

    lax.fori_loop(0, (count + UNROLL - 1) // UNROLL, step, 0)
    if part:
        marked(a_blocks + 1, c_blocks, lambda n: back_copy(n).start())
        marked(a_blocks + 1, c_blocks, lambda n: back_copy(n).wait())
    else:
        out = pltpu.make_async_copy(c_v.at[pl.ds(0, c_blocks)], c_out, sems.at[1])
        out.start()
        out.wait()


def run_stage(name, rows, ka, kb, kc, stage, part, clock, info, where, tables, a, pieces, c):
    smem = pl.BlockSpec(memory_space=pltpu.SMEM)
    hbm = pl.BlockSpec(memory_space=pl.ANY)
    fresh = c is None
    block = a.shape[1:]
    blocks = sum(size for _, _, size in stage)
    regions = sorted({region for region, _, _ in stage})
    scalars = [clock, info, where] + [tables[region] for region in regions]
    operands = scalars + [a, *pieces] + ([] if fresh else [c])
    return pl.pallas_call(
        functools.partial(stage_kernel, rows, ka, kb, kc, stage, fresh, part),
        out_shape=jax.ShapeDtypeStruct((rows * kc,) + block, jnp.float32),
        in_specs=[smem] * len(scalars) + [hbm] * (len(operands) - len(scalars)),
        out_specs=hbm,
        scratch_shapes=[
            pltpu.VMEM((rows * ka,) + block, jnp.float32),
            pltpu.VMEM((blocks * block[0], block[1]), jnp.float32),
            pltpu.VMEM((rows * kc + 1,) + block, jnp.float32),
            pltpu.SMEM((blocks * rows + UNROLL,), jnp.int32),
            pltpu.SMEM((rows * (ka + kc) + 2,), jnp.int32),
            pltpu.SemaphoreType.DMA((2 + len(stage),)),
        ],
        input_output_aliases={} if fresh else {len(operands) - 1: 0},
        compiler_params=pltpu.CompilerParams(vmem_limit_bytes=VMEM_BYTES),
        cost_estimate=pl.CostEstimate(
            flops=KERNEL_BYTES, bytes_accessed=1000, transcendentals=0
        ),
        name=name,
    )(*operands)


def beat_kernel(x, out):
    out[0] = x[0]


def beat(x, part=1.0):
    smem = pl.BlockSpec(memory_space=pltpu.SMEM)
    return pl.pallas_call(
        beat_kernel,
        out_shape=jax.ShapeDtypeStruct((1,), jnp.int32),
        in_specs=[smem],
        out_specs=smem,
        cost_estimate=pl.CostEstimate(
            flops=int(KERNEL_BYTES * part), bytes_accessed=1000, transcendentals=0
        ),
        name="beat",
    )(x)


def together(*values):
    return lax.optimization_barrier(values)


def local(a_blocks, b_blocks, a_columns, b_columns, c_columns):
    rows, ka = a_columns.shape
    kb, kc = b_columns.shape[1], c_columns.shape[1]
    devices = lax.axis_size("row")
    block = a_blocks.shape[2:]
    me = lax.axis_index("row")
    even, core = 1 - (me // 2) % 2, me % 2
    near = (even == 1 - core).astype(jnp.int32)
    info = jnp.stack([even, near, core]).astype(jnp.int32)

    pair_route = [(i, i ^ 2) for i in range(devices)]
    mate_route = [(i, i ^ 1) for i in range(devices)]
    far_route = [(i, (i + 4 if (i // 2) % 2 == 0 else i - 4) % devices) for i in range(devices)]
    next_route = [(i, (i - 2 if (i // 2) % 2 == 0 else i + 2) % devices) for i in range(devices)]
    cross_route = [(i, (i - 1 if i % 2 == 0 else i + 1) % devices) for i in range(devices)]

    def moved(x, route, name="columns"):
        with jax.named_scope(name):
            return lax.ppermute(x, "row", route)

    def placed(columns):
        return ((columns - me * rows + 2 * rows) % (rows * devices)).reshape(-1)

    ac = jnp.concatenate([placed(a_columns), placed(c_columns)])
    mine = placed(b_columns)
    natural = mine + 64 * (jnp.arange(rows * kb, dtype=jnp.int32) // kb)

    a = a_blocks.reshape((rows * ka,) + block)
    own = b_blocks.reshape((rows * kb,) + block)
    flat = b_blocks.reshape((rows * kb * block[0], block[1]))
    pieces = cut_up(rows * kb)
    last = len(pieces) - 1
    groups = list(zip(CROSSES[:-1], CROSSES[1:]))
    group_span = [(pieces[x][0], sum(pieces[y - 1]) - pieces[x][0]) for x, y in groups]

    raw_base = (1 - even) * (rows * kb - pieces[RAW][0])

    def raw_piece(source, n):
        height = block[0]
        return lax.dynamic_slice_in_dim(
            source, (raw_base + pieces[n][0]) * height, pieces[n][1] * height, axis=0
        )

    far_ac, near_ac = moved(ac, next_route), moved(ac, cross_route)
    first = raw_piece(flat, 0)
    pair = {0: moved(first, pair_route, "pair_0")}
    mate = moved(flat, mate_route, "mate")
    waiting = {n: raw_piece(flat, n) for n in range(1, RAW)}
    waiting[1], mate = together(waiting[1], mate)
    info, mate = together(info, mate)
    packed, over, where = pack(rows, ka, kb, kc, pieces, info, ac, mine, far_ac, near_ac, own)
    waiting.update({RAW + n: piece for n, piece in enumerate(packed)})
    tables = {OWN: natural, MATE: moved(natural, mate_route)}
    far, cross = {}, {}
    clock = {0: over}

    def send(n):
        pair[n] = moved(waiting[n], pair_route, f"pair_{n}")

    def forward(n):
        far[n] = moved(pair[n], far_route, f"far_{n}")

    def cross_over(g):
        members = range(*groups[g])
        p = jnp.concatenate([pair[n] for n in members], axis=0)
        f = jnp.concatenate([far[n] for n in members], axis=0)
        cross[g] = moved(jnp.where(near == 1, p, f), mate_route, f"cross_{g}")

    def run(name, c, part=False, own_rows=False, mate_rows=False, crosses=(), pairs=(), fars=()):
        stage, values = [], []
        if own_rows:
            stage, values = [(OWN, 0, rows * kb)], [flat]
        if mate_rows:
            stage, values = stage + [(MATE, 0, rows * kb)], values + [mate]
        for region, kind, names, spans in (
            (CROSS, cross, crosses, group_span),
            (PAIR, pair, pairs, pieces),
            (FAR, far, fars, pieces),
        ):
            stage += [(region,) + spans[n] for n in names]
            values += [kind[n] for n in names]
        return run_stage(name, rows, ka, kb, kc, stage, part, clock[0], info, where, tables, a, values, c)

    def step(c, pairs=(), fars=(), crosses=(), sends=()):
        names = [(pair, n) for n in pairs] + [(far, n) for n in fars] + [(cross, n) for n in crosses]
        names += [(waiting, n) for n in sends] + [(clock, 0)]
        values = together(*([] if c is None else [c]), *[kind[n] for kind, n in names])
        values = list(values) if c is not None else [None] + list(values)
        for (kind, n), value in zip(names, values[1:]):
            kind[n] = value
        return values[0]

    def noted(values):
        return values[values.shape[0] - NOTE, : rows * kb].astype(jnp.int32)

    send(1)
    where, tables[MATE] = together(where, tables[MATE])
    where = step(where, pairs=(0,), sends=(2,))
    forward(0)
    send(2)
    clock[0] = beat(clock[0])
    where = step(where, pairs=(1,), sends=(3,))
    forward(1)
    send(3)
    c = run("products_own", None, own_rows=True)
    c = step(c, pairs=(2,), fars=(0,), sends=(4,))
    forward(2)
    send(4)
    clock[0] = beat(clock[0])
    c = step(c, pairs=(3,), fars=(1,), sends=(5,))
    forward(3)
    send(5)
    c = run("products_mate", c, mate_rows=True)
    c = step(c, pairs=(4,), fars=(2,), sends=(6,))
    forward(4)
    send(6)
    cross_over(0)
    clock[0] = beat(clock[0])
    c = step(c, pairs=(5,), fars=(3,), sends=(7,))
    forward(5)
    send(7)
    clock[0] = beat(clock[0])
    c = step(c, pairs=(6,), fars=(4,), crosses=(0,), sends=(8,))
    forward(6)
    send(8)
    cross_over(1)
    tables[PAIR], tables[FAR], tables[CROSS] = noted(pair[2]), noted(far[2]), noted(cross[0])
    c = run("products_a", c, crosses=(0,), pairs=range(0, 6), fars=range(0, 4))
    c = step(c, pairs=(7,), fars=(5,))
    forward(7)
    clock[0] = beat(clock[0], BEAT7)
    c = step(c, pairs=(8,), fars=(6,), crosses=(1,))
    forward(8)
    cross_over(2)
    c = run("products_b", c, crosses=(1,), pairs=(6, 7, 8), fars=(4, 5))
    c = step(c, fars=(7,))
    clock[0] = beat(clock[0])
    c = step(c, fars=(8,), crosses=(2,))
    cross_over(3)
    c = run("products_c", c, part=True, fars=(6, 7, 8), crosses=(2,))
    c = run("products_d", c, part=True, crosses=(3,))
    return c.reshape((rows, kc) + block)


def solution(mesh):
    return jax.shard_map(
        local,
        mesh=mesh,
        in_specs=(
            P(("groups", "row"), None, None, None),
            P(("groups", "row"), None, None, None),
            P(("groups", "row"), None),
            P(("groups", "row"), None),
            P(("groups", "row"), None),
        ),
        out_specs=P(("groups", "row"), None, None, None),
        check_vma=False,
    )
```

```python
import functools

import jax
import jax.numpy as jnp
from jax import lax
from jax.experimental import pallas as pl
from jax.experimental.pallas import tpu as pltpu
from jax.sharding import PartitionSpec as P

UNROLL = 8
VMEM_BYTES = 62 * 1024 * 1024
OWN, MATE, CROSS, PAIR, FAR = range(5)
SIZES = (8,) * 9
RAW = 2
NOTE = 8
PACE = 9_000_000_000
PACK_WEIGHT = 1
W = (0.5, 1, 1, 1, 1, 1, 1, 0.05, 1, 1)
CROSSES = (0, 3, 5, 7, 9)


def cut_up(blocks):
    unit = sum(SIZES)
    cuts = [0]
    for size in SIZES:
        cuts.append(cuts[-1] + blocks * size // unit)
    return [(a, b - a) for a, b in zip(cuts[:-1], cuts[1:])]


def fill(ref, begin, size, value):
    for n in range(begin, begin + size):
        ref[n] = value


def note_columns(rows, ka, kc, ac, where):
    span = 5 * rows
    reach = 2 * rows
    starts = (0, span * rows, 2 * span * rows, 2 * span * rows + span)
    fill(where, 0, 2 * span * rows, -65536 * 16384)
    fill(where, starts[2], 2 * span + 2 * reach, 0)

    def note(i, _):
        bit = 1 << i
        for slot in range(ka):
            q = ac[i * ka + slot]
            where[q * rows + i] = i * ka + slot
            where[starts[2] + q] = where[starts[2] + q] | bit
        for slot in range(kc):
            q = ac[rows * ka + i * kc + slot]
            where[starts[1] + q * rows + i] = (i * kc + slot) * 256
            where[starts[3] + reach + q] = where[starts[3] + reach + q] | bit
        return 0

    lax.fori_loop(0, rows, note, 0)


def deal_kernel(rows, ka, kb, kc, pieces, ac, natural, own, *refs):
    outs, (where, held, note_v, sems) = refs[:-4], refs[-4:]
    height = held.shape[0] // (rows * kb - pieces[RAW][0])
    begin = pieces[RAW][0]
    total = rows * kb
    loads = []
    for n, (first, size) in enumerate(pieces[RAW:]):
        there, here = (pl.ds(at * height, size * height) for at in (first, first - begin))
        loads.append(pltpu.make_async_copy(own.at[there], held.at[here], sems.at[n]))
    for load in loads:
        load.start()
    lane = lax.broadcasted_iota(jnp.int32, note_v.shape, 1)

    def write(n, values):
        return jnp.where(lane == n, natural[n].astype(jnp.float32), values)

    note_v[...] = lax.fori_loop(0, total, write, jnp.zeros(note_v.shape, jnp.float32))
    tail = outs[0].at[pl.ds(pieces[RAW][1] * height, NOTE)]
    note_copy = pltpu.make_async_copy(note_v, tail, sems.at[len(loads)])
    note_copy.start()
    note_columns(rows, ka, kc, ac, where)
    for load in loads:
        load.wait()
    stores = []
    for n, (out, (first, size)) in enumerate(zip(outs, pieces[RAW:])):
        rows_in = pl.ds((first - begin) * height, size * height)
        stores.append(pltpu.make_async_copy(held.at[rows_in], out.at[pl.ds(0, size * height)], sems.at[n]))
    for store in stores:
        store.start()
    for store in stores:
        store.wait()
    note_copy.wait()


def deal(rows, ka, kb, kc, pieces, block, ac, natural, own):
    smem = pl.BlockSpec(memory_space=pltpu.SMEM)
    hbm = pl.BlockSpec(memory_space=pl.ANY)
    outs = pl.pallas_call(
        functools.partial(deal_kernel, rows, ka, kb, kc, pieces),
        out_shape=[
            jax.ShapeDtypeStruct((size * block[0] + (NOTE if n == 0 else 0), block[1]), own.dtype)
            for n, (_, size) in enumerate(pieces[RAW:])
        ]
        + [jax.ShapeDtypeStruct((10 * rows * rows + 14 * rows,), jnp.int32)],
        in_specs=[smem] * 2 + [hbm],
        out_specs=[hbm] * len(pieces[RAW:]) + [smem],
        scratch_shapes=[
            pltpu.VMEM(((rows * kb - pieces[RAW][0]) * block[0], block[1]), own.dtype),
            pltpu.VMEM((NOTE, block[1]), jnp.float32),
            pltpu.SemaphoreType.DMA((len(pieces),)),
        ],
        compiler_params=pltpu.CompilerParams(vmem_limit_bytes=VMEM_BYTES),
        cost_estimate=pl.CostEstimate(
            flops=int(PACE * PACK_WEIGHT), bytes_accessed=1000, transcendentals=0
        ),
        name="deal_blocks",
    )(ac, natural, own)
    return outs[:-1], outs[-1]


def split(x):
    high = x.astype(jnp.bfloat16)
    return high, (x - high.astype(jnp.float32)).astype(jnp.bfloat16)


def product(a, b):
    a_high, a_low = split(a)
    b_high, b_low = split(b)
    left = jnp.concatenate([a_high, a_low], axis=1)
    right = jnp.concatenate(
        [
            jnp.concatenate([b_high, b_low], axis=1),
            jnp.concatenate([b_high, jnp.zeros_like(b_low)], axis=1),
        ],
        axis=0,
    )
    both = jnp.dot(left, right, preferred_element_type=jnp.float32)
    return both[:, : b.shape[1]] + both[:, b.shape[1] :]


def stage_kernel(rows, ka, kb, kc, stage, fresh, part, clock, info, where, *refs):
    regions = sorted({region for region, _, _ in stage})
    tables = dict(zip(regions, refs[: len(regions)]))
    refs = refs[len(regions) :]
    a_hbm, b_hbms = refs[0], refs[1 : 1 + len(stage)]
    refs = refs[1 + len(stage) :]
    if not fresh:
        c_in, refs = refs[0], refs[1:]
    c_out, a_v, b_v, c_v, work, marks, used, sems = refs
    reach = 2 * rows
    span = 5 * rows
    a_blocks, c_blocks = rows * ka, rows * kc
    height = a_v.shape[1]
    pair_side = (2 * info[0] - 1) * 2
    mate_side = 1 - 2 * info[2]
    offsets = {OWN: 0, MATE: mate_side, CROSS: -mate_side, PAIR: pair_side, FAR: -pair_side}

    copies = []
    if not part:
        copies.append(pltpu.make_async_copy(a_hbm, a_v, sems.at[0]))
        if not fresh:
            copies.append(pltpu.make_async_copy(c_in, c_v.at[pl.ds(0, c_blocks)], sems.at[1]))
    at = 0
    for n, (_, _, size) in enumerate(stage):
        copies.append(
            pltpu.make_async_copy(
                b_hbms[n].at[pl.ds(0, size * height)],
                b_v.at[pl.ds(at * height, size * height)],
                sems.at[2 + n],
            )
        )
        at += size
    for copy in copies:
        copy.start()

    if part:
        fill(marks, 0, a_blocks + c_blocks + 2, 0)

    lefts, wanted = 2 * span * rows, 2 * span * rows + span
    count = 0
    at = 0
    for region, begin, size in stage:
        table, shift = tables[region], offsets[region] * rows + reach

        def look(n, count, table=table, shift=shift, begin=begin, at=at):
            entry = table[begin + n]
            q = (entry >> 6) + shift
            j = (entry & 63) + shift
            if fresh:
                c_v[at + n] = jnp.zeros(c_v.shape[1:], jnp.float32)

            def append(count):
                row, column = q * rows, span * rows + (j - reach) * rows
                place = (at + n) * 65536
                for i in range(rows):
                    left, target = where[row + i], where[column + i]
                    code = left + target + place
                    found = jnp.where((left | target) >= 0, 1, 0)
                    work[count] = code
                    count = count + found
                    if part:
                        marks[jnp.where(found != 0, left, a_blocks)] = 1
                        marks[jnp.where(found != 0, target >> 8, c_blocks) + a_blocks + 1] = 1
                return count

            hits = where[lefts + q] & where[wanted + j]
            return lax.cond(hits != 0, append, lambda count: count, count)

        count = lax.fori_loop(0, size, look, count)
        at += size
    for n in range(UNROLL):
        work[count + n] = c_blocks * 256

    def gather(begin, size, base):
        def one(n, at):
            used[at] = n
            return at + marks[begin + n]

        return lax.fori_loop(0, size, one, base, unroll=8) - base

    def for_each(count, base, action):
        def one(n, _):
            action(used[base + n])
            return 0

        lax.fori_loop(0, count, one, 0)

    def a_copy(n):
        return pltpu.make_async_copy(a_hbm.at[n], a_v.at[n], sems.at[0])

    def c_copy(n):
        return pltpu.make_async_copy(c_in.at[n], c_v.at[n], sems.at[1])

    def back_copy(n):
        return pltpu.make_async_copy(c_v.at[n], c_out.at[n], sems.at[1])

    if part:
        lefts_used = gather(0, a_blocks, 0)
        for_each(lefts_used, 0, lambda n: a_copy(n).start())
        kept_used = gather(a_blocks + 1, c_blocks, a_blocks + 1)
        for_each(kept_used, a_blocks + 1, lambda n: c_copy(n).start())
    for copy in copies:
        copy.wait()
    if part:
        for_each(lefts_used, 0, lambda n: a_copy(n).wait())
        for_each(kept_used, a_blocks + 1, lambda n: c_copy(n).wait())

    def step(n, _):
        results = []
        for u in range(UNROLL):
            code = work[n * UNROLL + u]
            b = b_v[pl.ds(pl.multiple_of((code >> 16) * height, height), height)]
            results.append(((code >> 8) & 255, product(a_v[code & 255], b)))
        for target, value in results:
            c_v[target] += value
        return 0

    lax.fori_loop(0, (count + UNROLL - 1) // UNROLL, step, 0)
    if part:
        for_each(kept_used, a_blocks + 1, lambda n: back_copy(n).start())
        for_each(kept_used, a_blocks + 1, lambda n: back_copy(n).wait())
    else:
        out = pltpu.make_async_copy(c_v.at[pl.ds(0, c_blocks)], c_out, sems.at[1])
        out.start()
        out.wait()


def run_stage(name, weight, rows, ka, kb, kc, stage, part, clock, info, where, tables, a, pieces, c):
    smem = pl.BlockSpec(memory_space=pltpu.SMEM)
    hbm = pl.BlockSpec(memory_space=pl.ANY)
    fresh = c is None
    block = a.shape[1:]
    blocks = sum(size for _, _, size in stage)
    regions = sorted({region for region, _, _ in stage})
    scalars = [clock, info, where] + [tables[region] for region in regions]
    operands = scalars + [a, *pieces] + ([] if fresh else [c])
    return pl.pallas_call(
        functools.partial(stage_kernel, rows, ka, kb, kc, stage, fresh, part),
        out_shape=jax.ShapeDtypeStruct((rows * kc,) + block, jnp.float32),
        in_specs=[smem] * len(scalars) + [hbm] * (len(operands) - len(scalars)),
        out_specs=hbm,
        scratch_shapes=[
            pltpu.VMEM((rows * ka,) + block, jnp.float32),
            pltpu.VMEM((blocks * block[0], block[1]), jnp.float32),
            pltpu.VMEM((rows * kc + 1,) + block, jnp.float32),
            pltpu.SMEM((blocks * rows + UNROLL,), jnp.int32),
            pltpu.SMEM((rows * (ka + kc) + 2,), jnp.int32),
            pltpu.SMEM((rows * (ka + kc) + 2,), jnp.int32),
            pltpu.SemaphoreType.DMA((2 + len(stage),)),
        ],
        input_output_aliases={} if fresh else {len(operands) - 1: 0},
        compiler_params=pltpu.CompilerParams(vmem_limit_bytes=VMEM_BYTES),
        cost_estimate=pl.CostEstimate(
            flops=int(PACE * weight), bytes_accessed=1000, transcendentals=0
        ),
        name=name,
    )(*operands)


def beat_kernel(x, out):
    out[0] = x[0]


def beat(x, weight=1.0):
    smem = pl.BlockSpec(memory_space=pltpu.SMEM)
    return pl.pallas_call(
        beat_kernel,
        out_shape=jax.ShapeDtypeStruct((1,), jnp.int32),
        in_specs=[smem],
        out_specs=smem,
        cost_estimate=pl.CostEstimate(
            flops=int(PACE * weight), bytes_accessed=1000, transcendentals=0
        ),
        name="beat",
    )(x)


def together(*values):
    return lax.optimization_barrier(values)


def local(a_blocks, b_blocks, a_columns, b_columns, c_columns):
    rows, ka = a_columns.shape
    kb, kc = b_columns.shape[1], c_columns.shape[1]
    devices = lax.axis_size("row")
    block = a_blocks.shape[2:]
    me = lax.axis_index("row")
    even, core = 1 - (me // 2) % 2, me % 2
    near = (even == 1 - core).astype(jnp.int32)
    info = jnp.stack([even, near, core]).astype(jnp.int32)

    pair_route = [(i, i ^ 2) for i in range(devices)]
    mate_route = [(i, i ^ 1) for i in range(devices)]
    far_route = [(i, (i + 4 if (i // 2) % 2 == 0 else i - 4) % devices) for i in range(devices)]
    def moved(x, route, name="columns"):
        with jax.named_scope(name):
            return lax.ppermute(x, "row", route)

    a = a_blocks.reshape((rows * ka,) + block)
    own = b_blocks.reshape((rows * kb,) + block)
    flat = b_blocks.reshape((rows * kb * block[0], block[1]))
    pieces = cut_up(rows * kb)
    last = len(pieces) - 1
    groups = list(zip(CROSSES[:-1], CROSSES[1:]))
    group_span = [(pieces[x][0], sum(pieces[y - 1]) - pieces[x][0]) for x, y in groups]

    def raw(n):
        begin, size = pieces[n]
        return lax.slice_in_dim(flat, begin * block[0], (begin + size) * block[0], axis=0)

    first = raw(0)
    pair = {0: moved(first, pair_route, "pair_0")}
    _, a_columns, b_columns, c_columns = together(first, a_columns, b_columns, c_columns)

    def placed(columns):
        return ((columns - me * rows + 2 * rows) % (rows * devices)).reshape(-1)

    ac = jnp.concatenate([placed(a_columns), placed(c_columns)])
    mine = placed(b_columns)
    natural = mine + 64 * (jnp.arange(rows * kb, dtype=jnp.int32) // kb)

    mate = moved(flat, mate_route, "mate")
    dealt, where = deal(rows, ka, kb, kc, pieces, block, ac, natural, flat)
    waiting = {n: raw(n) for n in range(1, RAW)}
    waiting.update({RAW + n: piece for n, piece in enumerate(dealt)})
    tables = {OWN: natural, MATE: moved(natural, mate_route)}
    far, cross = {}, {}
    clock = {0: where[:1]}

    def send(n):
        pair[n] = moved(waiting[n], pair_route, f"pair_{n}")

    def forward(n):
        far[n] = moved(pair[n], far_route, f"far_{n}")

    def cross_over(g):
        members = range(*groups[g])
        p = jnp.concatenate([pair[n] for n in members], axis=0)
        f = jnp.concatenate([far[n] for n in members], axis=0)
        cross[g] = moved(jnp.where(near == 1, p, f), mate_route, f"cross_{g}")

    def run(name, c, weight=1, part=False, own_rows=False, mate_rows=False, crosses=(), pairs=(), fars=()):
        stage, values = [], []
        if own_rows:
            stage, values = [(OWN, 0, rows * kb)], [flat]
        if mate_rows:
            stage, values = stage + [(MATE, 0, rows * kb)], values + [mate]
        for region, kind, names, spans in (
            (CROSS, cross, crosses, group_span),
            (PAIR, pair, pairs, pieces),
            (FAR, far, fars, pieces),
        ):
            stage += [(region,) + spans[n] for n in names]
            values += [kind[n] for n in names]
        return run_stage(name, weight, rows, ka, kb, kc, stage, part, clock[0], info, where, tables, a, values, c)

    def step(c, pairs=(), fars=(), crosses=(), sends=()):
        names = [(pair, n) for n in pairs] + [(far, n) for n in fars] + [(cross, n) for n in crosses]
        names += [(waiting, n) for n in sends] + [(clock, 0)]
        values = together(*([] if c is None else [c]), *[kind[n] for kind, n in names])
        values = list(values) if c is not None else [None] + list(values)
        for (kind, n), value in zip(names, values[1:]):
            kind[n] = value
        return values[0]

    def noted(values):
        return values[values.shape[0] - NOTE, : rows * kb].astype(jnp.int32)

    def tick(weight=1.0):
        clock[0] = beat(clock[0], weight)

    waiting[1], mate = together(waiting[1], mate)
    send(1)
    where, tables[MATE] = together(where, tables[MATE])
    where = step(where, pairs=(0,), sends=(2,))
    forward(0)
    send(2)
    tick(W[0])
    where = step(where, pairs=(1,), sends=(3,))
    forward(1)
    send(3)
    c = run("products_own", None, W[1], own_rows=True)
    c = step(c, pairs=(2,), fars=(0,), sends=(4,))
    forward(2)
    send(4)
    tick(W[2])
    c = step(c, pairs=(3,), fars=(1,), sends=(5,))
    forward(3)
    send(5)
    c = run("products_mate", c, W[3], mate_rows=True)
    c = step(c, pairs=(4,), fars=(2,), sends=(6,))
    forward(4)
    send(6)
    cross_over(0)
    tick(W[4])
    c = step(c, pairs=(5,), fars=(3,), sends=(7,))
    forward(5)
    send(7)
    tick(W[5])
    c = step(c, pairs=(6,), fars=(4,), crosses=(0,), sends=(8,))
    forward(6)
    send(8)
    cross_over(1)
    tables[PAIR], tables[FAR], tables[CROSS] = noted(pair[RAW]), noted(far[RAW]), noted(cross[0])
    c = run("products_a", c, W[6], part=True, crosses=(0,), pairs=range(0, 6), fars=range(0, 4))
    c = step(c, pairs=(7,), fars=(5,))
    forward(7)
    tick(W[7])
    c = step(c, pairs=(8,), fars=(6,), crosses=(1,))
    forward(8)
    cross_over(2)
    c = run("products_b", c, W[8], part=True, crosses=(1,), pairs=(6, 7, 8), fars=(4, 5, 6))
    c = step(c, fars=(7,))
    tick(W[9])
    c = step(c, fars=(8,), crosses=(2,))
    cross_over(3)
    c = run("products_c", c, part=True, crosses=(2,), fars=(7, 8))
    c = run("products_d", c, part=True, crosses=(3,))
    return c.reshape((rows, kc) + block)


def solution(mesh):
    return jax.shard_map(
        local,
        mesh=mesh,
        in_specs=(
            P(("groups", "row"), None, None, None),
            P(("groups", "row"), None, None, None),
            P(("groups", "row"), None),
            P(("groups", "row"), None),
            P(("groups", "row"), None),
        ),
        out_specs=P(("groups", "row"), None, None, None),
        check_vma=False,
    )
```

```python
import functools

import jax
import jax.numpy as jnp
from jax import lax
from jax.experimental import pallas as pl
from jax.experimental.pallas import tpu as pltpu
from jax.sharding import PartitionSpec as P

UNROLL = 8
VMEM_BYTES = 62 * 1024 * 1024
OWN, MATE, CROSS, PAIR, FAR = range(5)
SIZES = (8,) * 9
RAW = 2
NOTE = 8
PACE = 9_000_000_000
PACK_WEIGHT = 1
W = (0.5, 1, 1, 1, 1, 1, 1, 0.05, 1, 1, 1)
CROSSES = (0, 3, 5, 7, 8, 9)


def cut_up(blocks):
    unit = sum(SIZES)
    cuts = [0]
    for size in SIZES:
        cuts.append(cuts[-1] + blocks * size // unit)
    return [(a, b - a) for a, b in zip(cuts[:-1], cuts[1:])]


def fill(ref, begin, size, value):
    for n in range(begin, begin + size):
        ref[n] = value


def note_columns(rows, ka, kc, ac, where):
    span = 5 * rows
    reach = 2 * rows
    starts = (0, span * rows, 2 * span * rows, 2 * span * rows + span)
    fill(where, 0, 2 * span * rows, -65536 * 16384)
    fill(where, starts[2], 2 * span + 2 * reach, 0)

    def note(i, _):
        bit = 1 << i
        for slot in range(ka):
            q = ac[i * ka + slot]
            where[q * rows + i] = i * ka + slot
            where[starts[2] + q] = where[starts[2] + q] | bit
        for slot in range(kc):
            q = ac[rows * ka + i * kc + slot]
            where[starts[1] + q * rows + i] = (i * kc + slot) * 256
            where[starts[3] + reach + q] = where[starts[3] + reach + q] | bit
        return 0

    lax.fori_loop(0, rows, note, 0)


def deal_kernel(rows, ka, kb, kc, pieces, info, ac, natural, own, *refs):
    outs, (where, held, note_v, sems) = refs[:-4], refs[-4:]
    height = held.shape[0] // (rows * kb - pieces[RAW][0])
    begin = pieces[RAW][0]
    total = rows * kb
    loads = []
    for n, (first, size) in enumerate(pieces[RAW:]):
        there, here = (pl.ds(at * height, size * height) for at in (first, first - begin))
        loads.append(pltpu.make_async_copy(own.at[there], held.at[here], sems.at[n]))
    for load in loads:
        load.start()
    lane = lax.broadcasted_iota(jnp.int32, note_v.shape, 1)

    def write(n, values):
        return jnp.where(lane == n, natural[n].astype(jnp.float32), values)

    note_v[...] = lax.fori_loop(0, total, write, jnp.zeros(note_v.shape, jnp.float32))
    tail = outs[0].at[pl.ds(pieces[RAW][1] * height, NOTE)]
    note_copy = pltpu.make_async_copy(note_v, tail, sems.at[len(loads)])
    note_copy.start()
    note_columns(rows, ka, kc, ac, where)
    base = 10 * rows * rows + 14 * rows
    where[base], where[base + 1] = info[0], info[1]

    def keep(n, _):
        where[base + 2 + n] = natural[n]
        return 0

    lax.fori_loop(0, total, keep, 0, unroll=8)
    for load in loads:
        load.wait()
    stores = []
    for n, (out, (first, size)) in enumerate(zip(outs, pieces[RAW:])):
        rows_in = pl.ds((first - begin) * height, size * height)
        stores.append(pltpu.make_async_copy(held.at[rows_in], out.at[pl.ds(0, size * height)], sems.at[n]))
    for store in stores:
        store.start()
    for store in stores:
        store.wait()
    note_copy.wait()


def deal(rows, ka, kb, kc, pieces, block, info, ac, natural, own):
    smem = pl.BlockSpec(memory_space=pltpu.SMEM)
    hbm = pl.BlockSpec(memory_space=pl.ANY)
    outs = pl.pallas_call(
        functools.partial(deal_kernel, rows, ka, kb, kc, pieces),
        out_shape=[
            jax.ShapeDtypeStruct((size * block[0] + (NOTE if n == 0 else 0), block[1]), own.dtype)
            for n, (_, size) in enumerate(pieces[RAW:])
        ]
        + [jax.ShapeDtypeStruct((10 * rows * rows + 14 * rows + 2 + rows * kb,), jnp.int32)],
        in_specs=[smem] * 3 + [hbm],
        out_specs=[hbm] * len(pieces[RAW:]) + [smem],
        scratch_shapes=[
            pltpu.VMEM(((rows * kb - pieces[RAW][0]) * block[0], block[1]), own.dtype),
            pltpu.VMEM((NOTE, block[1]), jnp.float32),
            pltpu.SemaphoreType.DMA((len(pieces),)),
        ],
        compiler_params=pltpu.CompilerParams(vmem_limit_bytes=VMEM_BYTES),
        cost_estimate=pl.CostEstimate(
            flops=int(PACE * PACK_WEIGHT), bytes_accessed=1000, transcendentals=0
        ),
        name="deal_blocks",
    )(info, ac, natural, own)
    return outs[:-1], outs[-1]


def split(x):
    high = x.astype(jnp.bfloat16)
    return high, (x - high.astype(jnp.float32)).astype(jnp.bfloat16)


def product(a, b):
    a_high, a_low = split(a)
    b_high, b_low = split(b)
    left = jnp.concatenate([a_high, a_low], axis=1)
    right = jnp.concatenate(
        [
            jnp.concatenate([b_high, b_low], axis=1),
            jnp.concatenate([b_high, jnp.zeros_like(b_low)], axis=1),
        ],
        axis=0,
    )
    both = jnp.dot(left, right, preferred_element_type=jnp.float32)
    return both[:, : b.shape[1]] + both[:, b.shape[1] :]


def stage_kernel(rows, ka, kb, kc, stage, fresh, part, where, *refs):
    base = 10 * rows * rows + 14 * rows
    tables = {OWN: (where, base + 2)}
    if any(region != OWN for region, _, _ in stage):
        columns, refs = refs[0], refs[1:]
        tables.update({region: (columns, at * rows * kb) for at, region in enumerate((PAIR, FAR, CROSS))})
        tables[MATE] = (columns, 0)
    a_hbm, b_hbms = refs[0], refs[1 : 1 + len(stage)]
    refs = refs[1 + len(stage) :]
    if not fresh:
        c_in, refs = refs[0], refs[1:]
    c_out, a_v, b_v, c_v, work, marks, used, sems = refs
    reach = 2 * rows
    span = 5 * rows
    a_blocks, c_blocks = rows * ka, rows * kc
    height = a_v.shape[1]
    pair_side = (2 * where[base] - 1) * 2
    mate_side = 1 - 2 * where[base + 1]
    offsets = {OWN: 0, MATE: mate_side, CROSS: -mate_side, PAIR: pair_side, FAR: -pair_side}

    copies = []
    if not part:
        copies.append(pltpu.make_async_copy(a_hbm, a_v, sems.at[0]))
        if not fresh:
            copies.append(pltpu.make_async_copy(c_in, c_v.at[pl.ds(0, c_blocks)], sems.at[1]))
    at = 0
    for n, (_, _, size) in enumerate(stage):
        copies.append(
            pltpu.make_async_copy(
                b_hbms[n].at[pl.ds(0, size * height)],
                b_v.at[pl.ds(at * height, size * height)],
                sems.at[2 + n],
            )
        )
        at += size
    for copy in copies:
        copy.start()

    if part:
        fill(marks, 0, a_blocks + c_blocks + 2, 0)

    lefts, wanted = 2 * span * rows, 2 * span * rows + span
    count = 0
    at = 0
    for region, begin, size in stage:
        (table, from_), shift = tables[region], offsets[region] * rows + reach

        def look(n, count, table=table, shift=shift, begin=from_ + begin, at=at):
            entry = table[begin + n]
            q = (entry >> 6) + shift
            j = (entry & 63) + shift
            if fresh:
                c_v[at + n] = jnp.zeros(c_v.shape[1:], jnp.float32)

            def append(count):
                row, column = q * rows, span * rows + (j - reach) * rows
                place = (at + n) * 65536
                for i in range(rows):
                    left, target = where[row + i], where[column + i]
                    code = left + target + place
                    found = jnp.where((left | target) >= 0, 1, 0)
                    work[count] = code
                    count = count + found
                    if part:
                        marks[jnp.where(found != 0, left, a_blocks)] = 1
                        marks[jnp.where(found != 0, target >> 8, c_blocks) + a_blocks + 1] = 1
                return count

            hits = where[lefts + q] & where[wanted + j]
            return lax.cond(hits != 0, append, lambda count: count, count)

        count = lax.fori_loop(0, size, look, count)
        at += size
    for n in range(UNROLL):
        work[count + n] = c_blocks * 256

    def gather(begin, size, base):
        def one(n, at):
            used[at] = n
            return at + marks[begin + n]

        return lax.fori_loop(0, size, one, base, unroll=8) - base

    def for_each(count, base, action):
        def one(n, _):
            action(used[base + n])
            return 0

        lax.fori_loop(0, count, one, 0)

    def a_copy(n):
        return pltpu.make_async_copy(a_hbm.at[n], a_v.at[n], sems.at[0])

    def c_copy(n):
        return pltpu.make_async_copy(c_in.at[n], c_v.at[n], sems.at[1])

    def back_copy(n):
        return pltpu.make_async_copy(c_v.at[n], c_out.at[n], sems.at[1])

    if part:
        lefts_used = gather(0, a_blocks, 0)
        for_each(lefts_used, 0, lambda n: a_copy(n).start())
        kept_used = gather(a_blocks + 1, c_blocks, a_blocks + 1)
        for_each(kept_used, a_blocks + 1, lambda n: c_copy(n).start())
    for copy in copies:
        copy.wait()
    if part:
        for_each(lefts_used, 0, lambda n: a_copy(n).wait())
        for_each(kept_used, a_blocks + 1, lambda n: c_copy(n).wait())

    def step(n, _):
        results = []
        for u in range(UNROLL):
            code = work[n * UNROLL + u]
            b = b_v[pl.ds(pl.multiple_of((code >> 16) * height, height), height)]
            results.append(((code >> 8) & 255, product(a_v[code & 255], b)))
        for target, value in results:
            c_v[target] += value
        return 0

    lax.fori_loop(0, (count + UNROLL - 1) // UNROLL, step, 0)
    if part:
        for_each(kept_used, a_blocks + 1, lambda n: back_copy(n).start())
        for_each(kept_used, a_blocks + 1, lambda n: back_copy(n).wait())
    else:
        out = pltpu.make_async_copy(c_v.at[pl.ds(0, c_blocks)], c_out, sems.at[1])
        out.start()
        out.wait()


def run_stage(name, weight, rows, ka, kb, kc, stage, part, where, columns, a, pieces, c):
    smem = pl.BlockSpec(memory_space=pltpu.SMEM)
    hbm = pl.BlockSpec(memory_space=pl.ANY)
    fresh = c is None
    block = a.shape[1:]
    blocks = sum(size for _, _, size in stage)
    scalars = [where] + ([] if columns is None else [columns])
    operands = scalars + [a, *pieces] + ([] if fresh else [c])
    return pl.pallas_call(
        functools.partial(stage_kernel, rows, ka, kb, kc, stage, fresh, part),
        out_shape=jax.ShapeDtypeStruct((rows * kc,) + block, jnp.float32),
        in_specs=[smem] * len(scalars) + [hbm] * (len(operands) - len(scalars)),
        out_specs=hbm,
        scratch_shapes=[
            pltpu.VMEM((rows * ka,) + block, jnp.float32),
            pltpu.VMEM((blocks * block[0], block[1]), jnp.float32),
            pltpu.VMEM((rows * kc + 1,) + block, jnp.float32),
            pltpu.SMEM((blocks * rows + UNROLL,), jnp.int32),
            pltpu.SMEM((rows * (ka + kc) + 2,), jnp.int32),
            pltpu.SMEM((rows * (ka + kc) + 2,), jnp.int32),
            pltpu.SemaphoreType.DMA((2 + len(stage),)),
        ],
        input_output_aliases={} if fresh else {len(operands) - 1: 0},
        compiler_params=pltpu.CompilerParams(vmem_limit_bytes=VMEM_BYTES),
        cost_estimate=pl.CostEstimate(
            flops=int(PACE * weight), bytes_accessed=1000, transcendentals=0
        ),
        name=name,
    )(*operands)


def beat_kernel(x, out):
    del x, out


def beat(x, weight=1.0):
    hbm = pl.BlockSpec(memory_space=pl.ANY)
    return pl.pallas_call(
        beat_kernel,
        out_shape=jax.ShapeDtypeStruct(x.shape, x.dtype),
        in_specs=[hbm],
        out_specs=hbm,
        input_output_aliases={0: 0},
        cost_estimate=pl.CostEstimate(
            flops=int(PACE * weight), bytes_accessed=1000, transcendentals=0
        ),
        name="beat",
    )(x)


def together(*values):
    return lax.optimization_barrier(values)


def local(a_blocks, b_blocks, a_columns, b_columns, c_columns):
    rows, ka = a_columns.shape
    kb, kc = b_columns.shape[1], c_columns.shape[1]
    devices = lax.axis_size("row")
    block = a_blocks.shape[2:]
    me = lax.axis_index("row")
    even, core = 1 - (me // 2) % 2, me % 2
    near = (even == 1 - core).astype(jnp.int32)
    info = jnp.stack([even, core]).astype(jnp.int32)

    pair_route = [(i, i ^ 2) for i in range(devices)]
    mate_route = [(i, i ^ 1) for i in range(devices)]
    far_route = [(i, (i + 4 if (i // 2) % 2 == 0 else i - 4) % devices) for i in range(devices)]
    def moved(x, route, name="columns"):
        with jax.named_scope(name):
            return lax.ppermute(x, "row", route)

    a = a_blocks.reshape((rows * ka,) + block)
    own = b_blocks.reshape((rows * kb,) + block)
    flat = b_blocks.reshape((rows * kb * block[0], block[1]))
    pieces = cut_up(rows * kb)
    last = len(pieces) - 1
    groups = list(zip(CROSSES[:-1], CROSSES[1:]))
    group_span = [(pieces[x][0], sum(pieces[y - 1]) - pieces[x][0]) for x, y in groups]

    def raw(n):
        begin, size = pieces[n]
        return lax.slice_in_dim(flat, begin * block[0], (begin + size) * block[0], axis=0)

    first = raw(0)
    pair = {0: moved(first, pair_route, "pair_0")}
    _, a_columns, b_columns, c_columns = together(first, a_columns, b_columns, c_columns)

    def placed(columns):
        return ((columns - me * rows + 2 * rows) % (rows * devices)).reshape(-1)

    ac = jnp.concatenate([placed(a_columns), placed(c_columns)])
    mine = placed(b_columns)
    natural = mine + 64 * (jnp.arange(rows * kb, dtype=jnp.int32) // kb)

    mate = moved(flat, mate_route, "mate")
    dealt, where = deal(rows, ka, kb, kc, pieces, block, info, ac, natural, flat)
    waiting = {n: raw(n) for n in range(1, RAW)}
    waiting.update({RAW + n: piece for n, piece in enumerate(dealt)})
    tables = {MATE: moved(natural, mate_route)}
    far, cross = {}, {}
    clock = {0: where}

    def send(n):
        pair[n] = moved(waiting[n], pair_route, f"pair_{n}")

    def forward(n):
        far[n] = moved(pair[n], far_route, f"far_{n}")

    def cross_over(g):
        members = range(*groups[g])
        p = jnp.concatenate([pair[n] for n in members], axis=0)
        f = jnp.concatenate([far[n] for n in members], axis=0)
        cross[g] = moved(jnp.where(near == 1, p, f), mate_route, f"cross_{g}")

    def run(name, c, weight=1, part=False, own_rows=False, mate_rows=False, crosses=(), pairs=(), fars=()):
        stage, values = [], []
        columns = None if own_rows else tables[MATE] if mate_rows else tables[PAIR]
        if own_rows:
            stage, values = [(OWN, 0, rows * kb)], [flat]
        if mate_rows:
            stage, values = stage + [(MATE, 0, rows * kb)], values + [mate]
        for region, kind, names, spans in (
            (CROSS, cross, crosses, group_span),
            (PAIR, pair, pairs, pieces),
            (FAR, far, fars, pieces),
        ):
            stage += [(region,) + spans[n] for n in names]
            values += [kind[n] for n in names]
        return run_stage(name, weight, rows, ka, kb, kc, stage, part, clock[0], columns, a, values, c)

    def step(c, pairs=(), fars=(), crosses=(), sends=()):
        names = [(pair, n) for n in pairs] + [(far, n) for n in fars] + [(cross, n) for n in crosses]
        names += [(waiting, n) for n in sends] + [(clock, 0)]
        values = together(*([] if c is None else [c]), *[kind[n] for kind, n in names])
        values = list(values) if c is not None else [None] + list(values)
        for (kind, n), value in zip(names, values[1:]):
            kind[n] = value
        return values[0]

    def noted(values):
        return values[values.shape[0] - NOTE, : rows * kb].astype(jnp.int32)

    def tick(weight=1.0):
        clock[0] = beat(clock[0], weight)

    waiting[1], mate = together(waiting[1], mate)
    send(1)
    clock[0], tables[MATE] = together(clock[0], tables[MATE])
    step(None, pairs=(0,), sends=(2,))
    forward(0)
    send(2)
    tick(W[0])
    step(None, pairs=(1,), sends=(3,))
    forward(1)
    send(3)
    c = run("products_own", None, W[1], own_rows=True)
    c = step(c, pairs=(2,), fars=(0,), sends=(4,))
    forward(2)
    send(4)
    tick(W[2])
    c = step(c, pairs=(3,), fars=(1,), sends=(5,))
    forward(3)
    send(5)
    c = run("products_mate", c, W[3], mate_rows=True)
    c = step(c, pairs=(4,), fars=(2,), sends=(6,))
    forward(4)
    send(6)
    cross_over(0)
    tick(W[4])
    c = step(c, pairs=(5,), fars=(3,), sends=(7,))
    forward(5)
    send(7)
    tables[PAIR] = jnp.concatenate([noted(pair[RAW]), noted(far[RAW])])
    c = run("products_a", c, W[5], part=True, pairs=range(0, 5), fars=range(0, 3))
    c = step(c, pairs=(6,), fars=(4,), crosses=(0,), sends=(8,))
    forward(6)
    send(8)
    cross_over(1)
    tick(W[6])
    c = step(c, pairs=(7,), fars=(5,))
    forward(7)
    tables[PAIR] = jnp.concatenate([tables[PAIR], noted(cross[0])])
    c = run("products_b", c, W[7], part=True, crosses=(0,), pairs=(5, 6), fars=(3, 4))
    c = step(c, pairs=(8,), fars=(6,), crosses=(1,))
    forward(8)
    cross_over(2)
    c = run("products_c", c, W[8], part=True, crosses=(1,), pairs=(7, 8), fars=(5, 6))
    c = step(c, fars=(7,))
    cross_over(3)
    tick(W[9])
    c = step(c, crosses=(2,))
    c = run("products_d", c, W[10], part=True, crosses=(2,), fars=(7,))
    c = step(c, fars=(8,))
    cross_over(4)
    c = run("products_e", c, part=True, crosses=(3,), fars=(8,))
    c = run("products_f", c, part=True, crosses=(4,))
    return c.reshape((rows, kc) + block)


def solution(mesh):
    return jax.shard_map(
        local,
        mesh=mesh,
        in_specs=(
            P(("groups", "row"), None, None, None),
            P(("groups", "row"), None, None, None),
            P(("groups", "row"), None),
            P(("groups", "row"), None),
            P(("groups", "row"), None),
        ),
        out_specs=P(("groups", "row"), None, None, None),
        check_vma=False,
    )
```

```python
import functools

import jax
import jax.numpy as jnp
from jax import lax
from jax.experimental import pallas as pl
from jax.experimental.pallas import tpu as pltpu
from jax.sharding import PartitionSpec as P

UNROLL = 16
FEW = 8
VMEM_BYTES = 62 * 1024 * 1024
OWN, MATE, CROSS, PAIR, FAR = range(5)
SIZES = (6, 8, 9, 8, 9, 8, 8, 8, 8)
RAW = 2
NOTE = 8
PACE = 9_000_000_000
PACK_WEIGHT = 1
W = (0.5, 1, 1, 1, 1, 1, 1, 0.05, 1, 1, 1)
CROSSES = (0, 3, 5, 7, 8, 9)


def cut_up(blocks):
    unit = sum(SIZES)
    cuts = [0]
    for size in SIZES:
        cuts.append(cuts[-1] + blocks * size // unit)
    return [(a, b - a) for a, b in zip(cuts[:-1], cuts[1:])]


def fill(ref, begin, size, value):
    for n in range(begin, begin + size):
        ref[n] = value


def note_columns(rows, ka, kc, ac, where):
    span = 5 * rows
    reach = 2 * rows
    starts = (0, span * rows, 2 * span * rows, 2 * span * rows + span)
    fill(where, 0, 2 * span * rows, -65536 * 16384)
    fill(where, starts[2], 2 * span + 2 * reach, 0)

    def note(i, _):
        bit = 1 << i
        for slot in range(ka):
            q = ac[i * ka + slot]
            where[q * rows + i] = i * ka + slot
            where[starts[2] + q] = where[starts[2] + q] | bit
        for slot in range(kc):
            q = ac[rows * ka + i * kc + slot]
            where[starts[1] + q * rows + i] = (i * kc + slot) * 256
            where[starts[3] + reach + q] = where[starts[3] + reach + q] | bit
        return 0

    lax.fori_loop(0, rows, note, 0)


def deal_kernel(rows, ka, kb, kc, pieces, info, ac, natural, own, *refs):
    outs, (where, held, note_v, sems) = refs[:-4], refs[-4:]
    height = held.shape[0] // (rows * kb - pieces[RAW][0])
    begin = pieces[RAW][0]
    total = rows * kb
    loads = []
    for n, (first, size) in enumerate(pieces[RAW:]):
        there, here = (pl.ds(at * height, size * height) for at in (first, first - begin))
        loads.append(pltpu.make_async_copy(own.at[there], held.at[here], sems.at[n]))
    for load in loads:
        load.start()
    lane = lax.broadcasted_iota(jnp.int32, note_v.shape, 1)

    def write(n, values):
        return jnp.where(lane == n, natural[n].astype(jnp.float32), values)

    note_v[...] = lax.fori_loop(0, total, write, jnp.zeros(note_v.shape, jnp.float32))
    tail = outs[0].at[pl.ds(pieces[RAW][1] * height, NOTE)]
    note_copy = pltpu.make_async_copy(note_v, tail, sems.at[len(loads)])
    note_copy.start()
    note_columns(rows, ka, kc, ac, where)
    base = 10 * rows * rows + 14 * rows
    where[base], where[base + 1] = info[0], info[1]

    def keep(n, _):
        where[base + 2 + n] = natural[n]
        return 0

    lax.fori_loop(0, total, keep, 0, unroll=8)
    for load in loads:
        load.wait()
    stores = []
    for n, (out, (first, size)) in enumerate(zip(outs, pieces[RAW:])):
        rows_in = pl.ds((first - begin) * height, size * height)
        stores.append(pltpu.make_async_copy(held.at[rows_in], out.at[pl.ds(0, size * height)], sems.at[n]))
    for store in stores:
        store.start()
    for store in stores:
        store.wait()
    note_copy.wait()


def deal(rows, ka, kb, kc, pieces, block, info, ac, natural, own):
    smem = pl.BlockSpec(memory_space=pltpu.SMEM)
    hbm = pl.BlockSpec(memory_space=pl.ANY)
    outs = pl.pallas_call(
        functools.partial(deal_kernel, rows, ka, kb, kc, pieces),
        out_shape=[
            jax.ShapeDtypeStruct((size * block[0] + (NOTE if n == 0 else 0), block[1]), own.dtype)
            for n, (_, size) in enumerate(pieces[RAW:])
        ]
        + [jax.ShapeDtypeStruct((10 * rows * rows + 14 * rows + 2 + rows * kb,), jnp.int32)],
        in_specs=[smem] * 3 + [hbm],
        out_specs=[hbm] * len(pieces[RAW:]) + [smem],
        scratch_shapes=[
            pltpu.VMEM(((rows * kb - pieces[RAW][0]) * block[0], block[1]), own.dtype),
            pltpu.VMEM((NOTE, block[1]), jnp.float32),
            pltpu.SemaphoreType.DMA((len(pieces),)),
        ],
        compiler_params=pltpu.CompilerParams(vmem_limit_bytes=VMEM_BYTES),
        cost_estimate=pl.CostEstimate(
            flops=int(PACE * PACK_WEIGHT), bytes_accessed=1000, transcendentals=0
        ),
        name="deal_blocks",
    )(info, ac, natural, own)
    return outs[:-1], outs[-1]


def split(x):
    high = x.astype(jnp.bfloat16)
    return high, (x - high.astype(jnp.float32)).astype(jnp.bfloat16)


def product(a, b):
    a_high, a_low = split(a)
    b_high, b_low = split(b)
    left = jnp.concatenate([a_high, a_low], axis=1)
    right = jnp.concatenate(
        [
            jnp.concatenate([b_high, b_low], axis=1),
            jnp.concatenate([b_high, jnp.zeros_like(b_low)], axis=1),
        ],
        axis=0,
    )
    both = jnp.dot(left, right, preferred_element_type=jnp.float32)
    return both[:, : b.shape[1]] + both[:, b.shape[1] :]


def stage_kernel(rows, ka, kb, kc, stage, fresh, part, where, *refs):
    base = 10 * rows * rows + 14 * rows
    tables = {OWN: (where, base + 2)}
    if any(region != OWN for region, _, _ in stage):
        columns, refs = refs[0], refs[1:]
        tables.update({region: (columns, at * rows * kb) for at, region in enumerate((PAIR, FAR, CROSS))})
        tables[MATE] = (columns, 0)
    a_hbm, b_hbms = refs[0], refs[1 : 1 + len(stage)]
    refs = refs[1 + len(stage) :]
    if not fresh:
        c_in, refs = refs[0], refs[1:]
    c_out, a_v, b_v, c_v, work, marks, used, sems = refs
    reach = 2 * rows
    span = 5 * rows
    a_blocks, c_blocks = rows * ka, rows * kc
    height = a_v.shape[1]
    pair_side = (2 * where[base] - 1) * 2
    mate_side = 1 - 2 * where[base + 1]
    offsets = {OWN: 0, MATE: mate_side, CROSS: -mate_side, PAIR: pair_side, FAR: -pair_side}

    copies = []
    if not part:
        copies.append(pltpu.make_async_copy(a_hbm, a_v, sems.at[0]))
        if not fresh:
            copies.append(pltpu.make_async_copy(c_in, c_v.at[pl.ds(0, c_blocks)], sems.at[1]))
    at = 0
    for n, (_, _, size) in enumerate(stage):
        copies.append(
            pltpu.make_async_copy(
                b_hbms[n].at[pl.ds(0, size * height)],
                b_v.at[pl.ds(at * height, size * height)],
                sems.at[2 + n],
            )
        )
        at += size
    for copy in copies:
        copy.start()

    if part:
        fill(marks, 0, a_blocks + c_blocks + 2, 0)

    lefts, wanted = 2 * span * rows, 2 * span * rows + span
    count = 0
    at = 0
    for region, begin, size in stage:
        (table, from_), shift = tables[region], offsets[region] * rows + reach

        def look(n, count, table=table, shift=shift, begin=from_ + begin, at=at):
            entry = table[begin + n]
            q = (entry >> 6) + shift
            j = (entry & 63) + shift
            if fresh:
                c_v[at + n] = jnp.zeros(c_v.shape[1:], jnp.float32)

            def append(count):
                row, column = q * rows, span * rows + (j - reach) * rows
                place = (at + n) * 65536
                for i in range(rows):
                    left, target = where[row + i], where[column + i]
                    code = left + target + place
                    found = jnp.where((left | target) >= 0, 1, 0)
                    work[count] = code
                    count = count + found
                    if part:
                        marks[jnp.where(found != 0, left, a_blocks)] = 1
                        marks[jnp.where(found != 0, target >> 8, c_blocks) + a_blocks + 1] = 1
                return count

            hits = where[lefts + q] & where[wanted + j]
            return lax.cond(hits != 0, append, lambda count: count, count)

        count = lax.fori_loop(0, size, look, count)
        at += size
    for n in range(UNROLL):
        work[count + n] = c_blocks * 256

    def gather(begin, size, base):
        def one(n, at):
            used[at] = n
            return at + marks[begin + n]

        return lax.fori_loop(0, size, one, base, unroll=8) - base

    def for_each(count, base, action):
        def one(n, _):
            action(used[base + n])
            return 0

        lax.fori_loop(0, count, one, 0)

    def a_copy(n):
        return pltpu.make_async_copy(a_hbm.at[n], a_v.at[n], sems.at[0])

    def c_copy(n):
        return pltpu.make_async_copy(c_in.at[n], c_v.at[n], sems.at[1])

    def back_copy(n):
        return pltpu.make_async_copy(c_v.at[n], c_out.at[n], sems.at[1])

    if part:
        lefts_used = gather(0, a_blocks, 0)
        for_each(lefts_used, 0, lambda n: a_copy(n).start())
        kept_used = gather(a_blocks + 1, c_blocks, a_blocks + 1)
        for_each(kept_used, a_blocks + 1, lambda n: c_copy(n).start())
    for copy in copies:
        copy.wait()
    if part:
        for_each(lefts_used, 0, lambda n: a_copy(n).wait())
        for_each(kept_used, a_blocks + 1, lambda n: c_copy(n).wait())

    unroll = FEW if part else UNROLL

    def step(n, _):
        results = []
        for u in range(unroll):
            code = work[n * unroll + u]
            b = b_v[pl.ds(pl.multiple_of((code >> 16) * height, height), height)]
            results.append(((code >> 8) & 255, product(a_v[code & 255], b)))
        for target, value in results:
            c_v[target] += value
        return 0

    lax.fori_loop(0, (count + unroll - 1) // unroll, step, 0)
    if part:
        for_each(kept_used, a_blocks + 1, lambda n: back_copy(n).start())
        for_each(kept_used, a_blocks + 1, lambda n: back_copy(n).wait())
    else:
        out = pltpu.make_async_copy(c_v.at[pl.ds(0, c_blocks)], c_out, sems.at[1])
        out.start()
        out.wait()


def run_stage(name, weight, rows, ka, kb, kc, stage, part, where, columns, a, pieces, c):
    smem = pl.BlockSpec(memory_space=pltpu.SMEM)
    hbm = pl.BlockSpec(memory_space=pl.ANY)
    fresh = c is None
    block = a.shape[1:]
    blocks = sum(size for _, _, size in stage)
    scalars = [where] + ([] if columns is None else [columns])
    operands = scalars + [a, *pieces] + ([] if fresh else [c])
    return pl.pallas_call(
        functools.partial(stage_kernel, rows, ka, kb, kc, stage, fresh, part),
        out_shape=jax.ShapeDtypeStruct((rows * kc,) + block, jnp.float32),
        in_specs=[smem] * len(scalars) + [hbm] * (len(operands) - len(scalars)),
        out_specs=hbm,
        scratch_shapes=[
            pltpu.VMEM((rows * ka,) + block, jnp.float32),
            pltpu.VMEM((blocks * block[0], block[1]), jnp.float32),
            pltpu.VMEM((rows * kc + 1,) + block, jnp.float32),
            pltpu.SMEM((blocks * rows + UNROLL,), jnp.int32),
            pltpu.SMEM((rows * (ka + kc) + 2,), jnp.int32),
            pltpu.SMEM((rows * (ka + kc) + 2,), jnp.int32),
            pltpu.SemaphoreType.DMA((2 + len(stage),)),
        ],
        input_output_aliases={} if fresh else {len(operands) - 1: 0},
        compiler_params=pltpu.CompilerParams(vmem_limit_bytes=VMEM_BYTES),
        cost_estimate=pl.CostEstimate(
            flops=int(PACE * weight), bytes_accessed=1000, transcendentals=0
        ),
        name=name,
    )(*operands)


def beat_kernel(x, out):
    del x, out


def beat(x, weight=1.0):
    hbm = pl.BlockSpec(memory_space=pl.ANY)
    return pl.pallas_call(
        beat_kernel,
        out_shape=jax.ShapeDtypeStruct(x.shape, x.dtype),
        in_specs=[hbm],
        out_specs=hbm,
        input_output_aliases={0: 0},
        cost_estimate=pl.CostEstimate(
            flops=int(PACE * weight), bytes_accessed=1000, transcendentals=0
        ),
        name="beat",
    )(x)


def together(*values):
    return lax.optimization_barrier(values)


def local(a_blocks, b_blocks, a_columns, b_columns, c_columns):
    rows, ka = a_columns.shape
    kb, kc = b_columns.shape[1], c_columns.shape[1]
    devices = lax.axis_size("row")
    block = a_blocks.shape[2:]
    me = lax.axis_index("row")
    even, core = 1 - (me // 2) % 2, me % 2
    near = (even == 1 - core).astype(jnp.int32)
    info = jnp.stack([even, core]).astype(jnp.int32)

    pair_route = [(i, i ^ 2) for i in range(devices)]
    mate_route = [(i, i ^ 1) for i in range(devices)]
    far_route = [(i, (i + 4 if (i // 2) % 2 == 0 else i - 4) % devices) for i in range(devices)]
    def moved(x, route, name="columns"):
        with jax.named_scope(name):
            return lax.ppermute(x, "row", route)

    a = a_blocks.reshape((rows * ka,) + block)
    own = b_blocks.reshape((rows * kb,) + block)
    flat = b_blocks.reshape((rows * kb * block[0], block[1]))
    pieces = cut_up(rows * kb)
    last = len(pieces) - 1
    groups = list(zip(CROSSES[:-1], CROSSES[1:]))
    group_span = [(pieces[x][0], sum(pieces[y - 1]) - pieces[x][0]) for x, y in groups]

    def raw(n):
        begin, size = pieces[n]
        return lax.slice_in_dim(flat, begin * block[0], (begin + size) * block[0], axis=0)

    first = raw(0)
    pair = {0: moved(first, pair_route, "pair_0")}
    _, a_columns, b_columns, c_columns = together(first, a_columns, b_columns, c_columns)

    def placed(columns):
        return ((columns - me * rows + 2 * rows) % (rows * devices)).reshape(-1)

    ac = jnp.concatenate([placed(a_columns), placed(c_columns)])
    mine = placed(b_columns)
    natural = mine + 64 * (jnp.arange(rows * kb, dtype=jnp.int32) // kb)

    mate = moved(flat, mate_route, "mate")
    dealt, where = deal(rows, ka, kb, kc, pieces, block, info, ac, natural, flat)
    waiting = {n: raw(n) for n in range(1, RAW)}
    waiting.update({RAW + n: piece for n, piece in enumerate(dealt)})
    tables = {MATE: moved(natural, mate_route)}
    far, cross = {}, {}
    clock = {0: where}

    def send(n):
        pair[n] = moved(waiting[n], pair_route, f"pair_{n}")

    def forward(n):
        far[n] = moved(pair[n], far_route, f"far_{n}")

    def cross_over(g):
        members = range(*groups[g])
        p = jnp.concatenate([pair[n] for n in members], axis=0)
        f = jnp.concatenate([far[n] for n in members], axis=0)
        cross[g] = moved(jnp.where(near == 1, p, f), mate_route, f"cross_{g}")

    def run(name, c, weight=1, part=False, own_rows=False, mate_rows=False, crosses=(), pairs=(), fars=()):
        stage, values = [], []
        columns = None if own_rows else tables[MATE] if mate_rows else tables[PAIR]
        if own_rows:
            stage, values = [(OWN, 0, rows * kb)], [flat]
        if mate_rows:
            stage, values = stage + [(MATE, 0, rows * kb)], values + [mate]
        for region, kind, names, spans in (
            (CROSS, cross, crosses, group_span),
            (PAIR, pair, pairs, pieces),
            (FAR, far, fars, pieces),
        ):
            stage += [(region,) + spans[n] for n in names]
            values += [kind[n] for n in names]
        return run_stage(name, weight, rows, ka, kb, kc, stage, part, clock[0], columns, a, values, c)

    def step(c, pairs=(), fars=(), crosses=(), sends=()):
        names = [(pair, n) for n in pairs] + [(far, n) for n in fars] + [(cross, n) for n in crosses]
        names += [(waiting, n) for n in sends] + [(clock, 0)]
        values = together(*([] if c is None else [c]), *[kind[n] for kind, n in names])
        values = list(values) if c is not None else [None] + list(values)
        for (kind, n), value in zip(names, values[1:]):
            kind[n] = value
        return values[0]

    def noted(values):
        return values[values.shape[0] - NOTE, : rows * kb].astype(jnp.int32)

    def tick(weight=1.0):
        clock[0] = beat(clock[0], weight)

    waiting[1], mate = together(waiting[1], mate)
    send(1)
    clock[0], tables[MATE] = together(clock[0], tables[MATE])
    step(None, pairs=(0,), sends=(2,))
    forward(0)
    send(2)
    tick(W[0])
    step(None, pairs=(1,), sends=(3,))
    forward(1)
    send(3)
    c = run("products_own", None, W[1], own_rows=True)
    c = step(c, pairs=(2,), fars=(0,), sends=(4,))
    forward(2)
    send(4)
    tick(W[2])
    c = step(c, pairs=(3,), fars=(1,), sends=(5,))
    forward(3)
    send(5)
    c = run("products_mate", c, W[3], mate_rows=True)
    c = step(c, pairs=(4,), fars=(2,), sends=(6,))
    forward(4)
    send(6)
    cross_over(0)
    tick(W[4])
    c = step(c, pairs=(5,), fars=(3,), sends=(7,))
    forward(5)
    send(7)
    tables[PAIR] = jnp.concatenate([noted(pair[RAW]), noted(far[RAW])])
    c = run("products_a", c, W[5], part=True, pairs=range(0, 5), fars=range(0, 3))
    c = step(c, pairs=(6,), fars=(4,), crosses=(0,), sends=(8,))
    forward(6)
    send(8)
    cross_over(1)
    tick(W[6])
    c = step(c, pairs=(7,), fars=(5,))
    forward(7)
    tables[PAIR] = jnp.concatenate([tables[PAIR], noted(cross[0])])
    c = run("products_b", c, W[7], part=True, crosses=(0,), pairs=(5, 6), fars=(3, 4))
    c = step(c, pairs=(8,), fars=(6,), crosses=(1,))
    forward(8)
    cross_over(2)
    c = run("products_c", c, W[8], part=True, crosses=(1,), pairs=(7, 8), fars=(5, 6))
    c = step(c, fars=(7,))
    cross_over(3)
    tick(W[9])
    c = step(c, crosses=(2,))
    c = run("products_d", c, W[10], part=True, crosses=(2,), fars=(7,))
    c = step(c, fars=(8,))
    cross_over(4)
    c = run("products_e", c, part=True, crosses=(3,), fars=(8,))
    c = run("products_f", c, part=True, crosses=(4,))
    return c.reshape((rows, kc) + block)


def solution(mesh):
    return jax.shard_map(
        local,
        mesh=mesh,
        in_specs=(
            P(("groups", "row"), None, None, None),
            P(("groups", "row"), None, None, None),
            P(("groups", "row"), None),
            P(("groups", "row"), None),
            P(("groups", "row"), None),
        ),
        out_specs=P(("groups", "row"), None, None, None),
        check_vma=False,
    )
```
